32 devices in a mesh: ctx: 8 (over y, x, core), fsdp: 4 (over z).
Axes of the slice: x: 2, y: 2, z: 4, core: 2. Of those that a mesh axis runs over, the one named last changes fastest.
Arguments:
- events: bfloat16 [2048, 4096], P('ctx'), may hold values from -6 to 6
- tile_mask: int32 [16, 2], P('ctx'), may hold values 0 or 1
- initial_state: float32 [4, 128, 128], P('fsdp'), may hold values from -96 to 96
- w_query: bfloat16 [4096, 512], P('ctx', 'fsdp'), may hold values from -0.09375 to 0.09375
- w_key: bfloat16 [4096, 512], P('ctx', 'fsdp'), may hold values from -0.09375 to 0.09375
- w_value: bfloat16 [4096, 512], P('ctx', 'fsdp'), may hold values from -0.09375 to 0.09375
- cotangent: bfloat16 [2048, 512], P('ctx', 'fsdp'), may hold values from -6 to 6
Outputs:
- attended: bfloat16 [2048, 512], P('ctx', 'fsdp')
- events_grad: bfloat16 [2048, 4096], P('ctx')
- query_grad: bfloat16 [4096, 512], P('ctx', 'fsdp')
- key_grad: bfloat16 [4096, 512], P('ctx', 'fsdp')
- value_grad: bfloat16 [4096, 512], P('ctx', 'fsdp')
The draws below stay inside these ranges and needn't reach their ends.
Inputs may be any that keep to these rules, and one draw needn't show every extreme that they name: `tile_mask`: only entries whose column is not above the row's tile place within its block of 256 events are read.
All inputs are finite; a program needn't handle non-finite values.
Results may differ from the reference program's by a relative error of at most 0.03.
Values may be sent and summed in bfloat16 or wider, within the bound.
A program may use at most 64 MiB of HBM per device.

```python
import jax
import jax.numpy as jnp
from jax import lax

D = 4096
HDIM = 128
HEAD_DEV = 1
HEADS = 4
TILE = 128
TOK_DEV = 256
TOKENS = 2048


def touch_ends(array, own_key, smallest, largest):
    longest = array.shape.index(max(array.shape))
    spots = []
    for shift in (0, 1):
        where = [jax.random.randint(jax.random.fold_in(own_key, axis), (), 0, length) for axis, length in enumerate(array.shape)]
        where[longest] = (where[longest] + shift) % array.shape[longest]
        spots.append(tuple(where))
    return array.at[spots[0]].set(smallest).at[spots[1]].set(largest)


def block_levels(own_key, extent, pieces, least, high):
    loudness, own = 1.0, jax.random.fold_in(own_key, 6)
    for axis_at, parts in pieces:
        heights = jnp.exp(jax.random.uniform(jax.random.fold_in(own, axis_at), (parts,), jnp.float32, least / len(pieces), high / len(pieces)))
        loudness = loudness * jnp.repeat(heights, extent[axis_at] // parts).reshape([-1 if axis == axis_at else 1 for axis in range(len(extent))])
    return loudness


def gaussian(own_key, dims, spread, reach, split=(), kind=jnp.bfloat16):
    factor_of = block_levels(own_key, dims, split, -0.22, 0.18) if split else 1.0
    array = jax.random.normal(own_key, dims, jnp.float32) * spread * factor_of
    return jnp.minimum(jnp.maximum(array, -reach), reach).astype(kind)


def setup_inputs(seed: int = 0) -> dict:
    keys = jax.random.split(jax.random.key(seed), 8)
    events = gaussian(keys[0], (TOKENS, D), 1.0, 6.0, ((0, 8),))
    tile_mask = touch_ends((jax.random.randint(keys[1], (TOKENS // TILE, TOK_DEV // TILE), 0, 4) < 3).astype(jnp.int32), jax.random.fold_in(keys[1], 1), 0, 1)
    initial_state = gaussian(keys[2], (HEADS, HDIM, HDIM), 16.0, 96.0, ((0, 4),), jnp.float32)
    w_query = gaussian(keys[3], (D, HEADS * HDIM), D ** -0.5, 0.09375, ((0, 8), (1, 4)))
    w_key = gaussian(keys[4], (D, HEADS * HDIM), D ** -0.5, 0.09375, ((0, 8), (1, 4)))
    w_value = gaussian(keys[5], (D, HEADS * HDIM), D ** -0.5, 0.09375, ((0, 8), (1, 4)))
    cotangent = gaussian(keys[6], (TOKENS, HEADS * HDIM), 1.0, 6.0, ((0, 8), (1, 4)))
    return dict(events=events, tile_mask=tile_mask, initial_state=initial_state, w_query=w_query, w_key=w_key, w_value=w_value, cotangent=cotangent)


epsilon = 1e-06

def allowed_pairs(mask_block, tile):
    count = mask_block.shape[0]
    size = count * tile
    row_index = lax.broadcasted_iota(jnp.int32, (size, size), 0)
    col_index = lax.broadcasted_iota(jnp.int32, (size, size), 1)
    tiled = jnp.repeat(jnp.repeat(mask_block, tile, axis=0), tile, axis=1)
    return jnp.where((col_index <= row_index) & (tiled > 0), 1.0, 0.0).astype(jnp.float32)

def block_forward(queries, key_rows, value_rows, carried_bf, allowed):
    scores = jnp.einsum('thd,shd->hts', queries.astype(jnp.float32), key_rows.astype(jnp.float32)) * allowed[None]
    mixing = scores.astype(jnp.bfloat16)
    mixture = jnp.einsum('hts,shd->thd', mixing.astype(jnp.float32), value_rows.astype(jnp.float32))
    mixture = mixture + jnp.einsum('thd,hde->the', queries.astype(jnp.float32), carried_bf.astype(jnp.float32))
    return (mixing, mixture)

def block_backward(queries, key_rows, value_rows, mixing, mixture_grad, carried_bf, later_bf, allowed):
    score_grad = (jnp.einsum('the,she->hts', mixture_grad.astype(jnp.float32), value_rows.astype(jnp.float32)) * allowed[None]).astype(jnp.bfloat16)
    sgrad = score_grad.astype(jnp.float32)
    query_part = jnp.einsum('hts,shd->thd', sgrad, key_rows.astype(jnp.float32))
    query_part = query_part + jnp.einsum('the,hde->thd', mixture_grad.astype(jnp.float32), carried_bf.astype(jnp.float32))
    key_part = jnp.einsum('hts,thd->shd', sgrad, queries.astype(jnp.float32))
    key_part = key_part + jnp.einsum('she,hde->shd', value_rows.astype(jnp.float32), later_bf.astype(jnp.float32))
    value_part = jnp.einsum('hts,the->she', mixing.astype(jnp.float32), mixture_grad.astype(jnp.float32))
    value_part = value_part + jnp.einsum('shd,hde->she', key_rows.astype(jnp.float32), later_bf.astype(jnp.float32))
    return (query_part.astype(jnp.bfloat16), key_part.astype(jnp.bfloat16), value_part.astype(jnp.bfloat16))

def reference(events, tile_mask, initial_state, w_query, w_key, w_value, cotangent):
    blocks = TOKENS // TOK_DEV
    count = TOK_DEV // TILE
    head_width = HEAD_DEV * HDIM
    groups = HEADS // HEAD_DEV
    masks = tile_mask.reshape(blocks, count, count)
    allowed = jax.vmap(lambda single: allowed_pairs(single, TILE))(masks)
    stacked = jnp.stack((w_query, w_key, w_value))
    event_blocks = events.reshape(blocks, TOK_DEV, D)

    def one_group(carry, index):
        start = (index * head_width).astype(jnp.int32)
        head_start = (index * HEAD_DEV).astype(jnp.int32)
        panels = lax.dynamic_slice_in_dim(stacked, start, head_width, 2)
        upstream_all = lax.dynamic_slice_in_dim(cotangent, start, head_width, 1)
        entering = lax.dynamic_slice_in_dim(initial_state, head_start, HEAD_DEV, 0)
        projected = [jnp.dot(events, panels[which], preferred_element_type=jnp.float32).astype(jnp.bfloat16) for which in range(3)]
        queries, key_rows, value_rows = [item.reshape(blocks, TOK_DEV, HEAD_DEV, HDIM) for item in projected]
        local_state = jnp.einsum('cthd,cthe->chde', key_rows.astype(jnp.float32), value_rows.astype(jnp.float32))
        running = jnp.cumsum(local_state, axis=0)
        zeros_state = jnp.zeros((1, HEAD_DEV, HDIM, HDIM), jnp.float32)
        carried = jnp.concatenate([zeros_state, running[:-1]], axis=0) + entering[None]
        carried_bf = carried.astype(jnp.bfloat16)
        mixing, mixture = jax.vmap(block_forward)(queries, key_rows, value_rows, carried_bf, allowed)
        inverse_rms = lax.rsqrt(lax.optimization_barrier(jnp.mean(mixture * mixture, axis=-1, keepdims=True)) + epsilon)
        attended = (mixture * inverse_rms).astype(jnp.bfloat16)
        upstream = upstream_all.reshape(blocks, TOK_DEV, HEAD_DEV, HDIM).astype(jnp.float32)
        mixture_grad = (inverse_rms * upstream - mixture * inverse_rms ** 3 * lax.optimization_barrier(jnp.mean(upstream * mixture, axis=-1, keepdims=True))).astype(jnp.bfloat16)
        local_grad = jnp.einsum('cthd,cthe->chde', queries.astype(jnp.float32), mixture_grad.astype(jnp.float32))
        backward_run = jnp.cumsum(local_grad[::-1], axis=0)[::-1]
        later = jnp.concatenate([backward_run[1:], zeros_state], axis=0)
        later_bf = later.astype(jnp.bfloat16)
        query_part, key_part, value_part = jax.vmap(block_backward)(queries, key_rows, value_rows, mixing, mixture_grad, carried_bf, later_bf, allowed)
        grads = jnp.stack([item.reshape(TOKENS, head_width) for item in (query_part, key_part, value_part)])
        term = jnp.einsum('ktw,kdw->td', grads.astype(jnp.float32), panels.astype(jnp.float32)).astype(jnp.bfloat16)
        carry = carry + term.astype(jnp.float32)
        grad_blocks = jnp.transpose(grads.reshape(3, blocks, TOK_DEV, head_width), (1, 0, 2, 3))

        def block_weight(pair):
            block_events, block_grads = pair
            return jnp.einsum('td,ktw->dkw', block_events.astype(jnp.float32), block_grads.astype(jnp.float32)).astype(jnp.bfloat16)
        weight_terms = lax.map(block_weight, (event_blocks, grad_blocks))
        weight_sum = lax.optimization_barrier(jnp.sum(weight_terms.astype(jnp.float32), axis=0)).astype(jnp.bfloat16)
        return (carry, (attended.reshape(TOKENS, head_width), weight_sum))
    initial = jnp.zeros((TOKENS, D), jnp.float32)
    total, (attended_all, weight_all) = lax.scan(one_group, initial, jnp.arange(groups, dtype=jnp.int32))
    attended_out = jnp.moveaxis(attended_all, 0, 1).reshape(TOKENS, HEADS * HDIM)
    outputs = []
    for which in range(3):
        outputs.append(jnp.moveaxis(weight_all[:, :, which, :], 0, 1).reshape(D, HEADS * HDIM))
    return (attended_out, total.astype(jnp.bfloat16), outputs[0], outputs[1], outputs[2])
```

```python
import jax
import jax.numpy as jnp
from jax import lax
from jax.experimental import pallas as pl
from jax.experimental.pallas import tpu as pltpu
from jax.sharding import PartitionSpec as P

HDIM = 128
TILE = 128


epsilon = 1e-06


def prefix(array, axis, combine, identity, reverse):
    count, index = (lax.axis_size(axis), lax.axis_index(axis))
    everything = lax.all_gather(array.astype(jnp.bfloat16), axis)
    start = jnp.broadcast_to(jnp.asarray(identity, array.dtype), array.shape)

    def turn(k, before):
        at = count - 1 - k if reverse else k
        reached = at > index if reverse else at < index
        new = combine(before, everything[at].astype(array.dtype))
        return jnp.where(reached, new, before)

    return lax.fori_loop(0, count, turn, start)


def allowed_pairs(mask_block, tile):
    count = mask_block.shape[0]
    size = count * tile
    row_index = lax.broadcasted_iota(jnp.int32, (size, size), 0)
    col_index = lax.broadcasted_iota(jnp.int32, (size, size), 1)
    tiled = jnp.repeat(jnp.repeat(mask_block, tile, axis=0), tile, axis=1)
    return jnp.where((col_index <= row_index) & (tiled > 0), 1.0, 0.0).astype(jnp.float32)


def add_states(earlier, later):
    return earlier + later


def block_prefix(local_term, reverse):
    return prefix(local_term, "ctx", add_states, jnp.zeros_like(local_term), reverse)


def on_device(events, tile_mask, initial_state, w_query, w_key, w_value, cotangent):
    event_count, head_width = cotangent.shape
    head_count = head_width // HDIM
    stacked = jnp.stack((w_query, w_key, w_value))
    allowed = allowed_pairs(tile_mask, TILE)
    panels = lax.all_gather(stacked, "ctx", axis=1, tiled=True)
    projected = jnp.einsum("td,kdw->ktw", events, panels, preferred_element_type=jnp.float32)
    projected = projected.astype(jnp.bfloat16).reshape(3, event_count, head_count, HDIM)
    queries, key_rows, value_rows = (projected[0], projected[1], projected[2])
    local_state = jnp.einsum(
        "thd,the->hde", key_rows, value_rows, preferred_element_type=jnp.float32
    )
    carried_bf = (block_prefix(local_state, False) + initial_state).astype(jnp.bfloat16)
    scores = (
        jnp.einsum("thd,shd->hts", queries, key_rows, preferred_element_type=jnp.float32)
        * allowed[None]
    )
    mixing = scores.astype(jnp.bfloat16)
    mixture = jnp.einsum("hts,shd->thd", mixing, value_rows, preferred_element_type=jnp.float32)
    mixture = mixture + jnp.einsum(
        "thd,hde->the", queries, carried_bf, preferred_element_type=jnp.float32
    )
    inverse_rms = lax.rsqrt(jnp.mean(mixture * mixture, axis=-1, keepdims=True) + epsilon)
    attended = (mixture * inverse_rms).astype(jnp.bfloat16).reshape(event_count, head_width)
    upstream = cotangent.reshape(event_count, head_count, HDIM).astype(jnp.float32)
    mixture_grad = (
        inverse_rms * upstream
        - mixture * inverse_rms**3 * jnp.mean(upstream * mixture, axis=-1, keepdims=True)
    ).astype(jnp.bfloat16)
    score_grad = (
        jnp.einsum("the,she->hts", mixture_grad, value_rows, preferred_element_type=jnp.float32)
        * allowed[None]
    ).astype(jnp.bfloat16)
    local_grad = jnp.einsum(
        "thd,the->hde", queries, mixture_grad, preferred_element_type=jnp.float32
    )
    later_bf = block_prefix(local_grad, True).astype(jnp.bfloat16)
    query_part = jnp.einsum(
        "hts,shd->thd", score_grad, key_rows, preferred_element_type=jnp.float32
    )
    query_part = query_part + jnp.einsum(
        "the,hde->thd", mixture_grad, carried_bf, preferred_element_type=jnp.float32
    )
    key_part = jnp.einsum("hts,thd->shd", score_grad, queries, preferred_element_type=jnp.float32)
    key_part = key_part + jnp.einsum(
        "she,hde->shd", value_rows, later_bf, preferred_element_type=jnp.float32
    )
    value_part = jnp.einsum(
        "hts,the->she", mixing, mixture_grad, preferred_element_type=jnp.float32
    )
    value_part = value_part + jnp.einsum(
        "shd,hde->she", key_rows, later_bf, preferred_element_type=jnp.float32
    )
    grads = (
        jnp.stack((query_part, key_part, value_part))
        .astype(jnp.bfloat16)
        .reshape(3, event_count, head_width)
    )
    partial_grad = jnp.einsum("ktw,kdw->td", grads, panels, preferred_element_type=jnp.float32)
    events_grad = lax.psum(partial_grad.astype(jnp.bfloat16), "fsdp")
    summed = lax.psum_scatter(
        jnp.einsum("td,ktw->dkw", events, grads, preferred_element_type=jnp.float32).astype(
            jnp.bfloat16
        ),
        "ctx",
        scatter_dimension=0,
        tiled=True,
    )
    return (attended, events_grad, summed[:, 0], summed[:, 1], summed[:, 2])


BF = jnp.bfloat16
F32 = jnp.float32
MESH = pl.DeviceIdType.MESH
ZN = 4


def mm(a, b, ca=1, cb=0):
    return lax.dot_general(a, b, (((ca,), (cb,)), ((), ())), preferred_element_type=F32)


def fused_kernel(
    ev_hbm, mask_ref, init_ref, wq_ref, wk_ref, wv_ref, cot_ref,
    att_ref, eg_ref, gq_ref, gk_ref, gv_ref,
    ev, evt, panels, st1, st2, zg, acc_ref,
    sib_out, sib_in, piece, xd, yd, xr, yr,
    ev_sem, ag_s, ag_r, st1_s, st1_r, st2_s, st2_r, rs_s, rs_r, zw_s, zw_r, zg_s, zg_r,
):
    depth = wq_ref.shape[0]
    half = depth // 2
    me = lax.axis_index("ctx")
    h = lax.axis_index("fsdp")
    core = me % 2
    xx = (me // 2) % 2
    yy = me // 4
    d1, d2, d4 = 1 - 2 * core, 2 - 4 * xx, 4 - 8 * yy
    peer = [me, me + d1, me + d2, me + d1 + d2, me + d4, me + d1 + d4, me + d2 + d4, me + d1 + d2 + d4]
    zpeer = [h, h + 1 - 2 * (h % 2), h + 2 - 4 * (h // 2), 3 - h]

    def copy(src, dst, ssem, rsem, target):
        return pltpu.make_async_remote_copy(
            src_ref=src, dst_ref=dst, send_sem=ssem, recv_sem=rsem, device_id=target, device_id_type=MESH
        )

    ev_copy = pltpu.make_async_copy(ev_hbm, ev, ev_sem)
    ev_copy.start()
    barrier = pltpu.get_barrier_semaphore()
    for r in range(1, 8):
        pl.semaphore_signal(barrier, inc=1, device_id={"ctx": peer[r]}, device_id_type=MESH)
    for z in range(1, ZN):
        pl.semaphore_signal(barrier, inc=1, device_id={"fsdp": zpeer[z]}, device_id_type=MESH)
    panels[0, :, 0:128] = wq_ref[...]
    panels[0, :, 128:256] = wk_ref[...]
    panels[0, :, 256:384] = wv_ref[...]
    pl.semaphore_wait(barrier, 10)

    rows = (pl.ds(0, half), pl.ds(half, half))

    def gather(z, k, slot, part, to_slot, via):
        return copy(
            panels.at[8 * z + slot, rows[part]],
            panels.at[8 * z + to_slot, rows[part]],
            ag_s.at[14 * z + k],
            ag_r.at[14 * z + k],
            {"ctx": peer[via]},
        )

    plan = (
        (0, 0, 2, 2), (0, 1, 2, 2), (0, 1, 4, 4), (0, 0, 4, 4), (0, 0, 1, 1), (0, 1, 1, 1), (2, 0, 6, 4), (4, 1, 6, 2),
        (2, 0, 3, 1), (2, 1, 3, 1), (4, 0, 5, 1), (4, 1, 5, 1), (6, 0, 7, 1), (6, 1, 7, 1),
    )
    moves = [[gather(z, k, *plan[k]) for k in range(14)] for z in range(ZN)]
    z_weights = [
        copy(panels.at[0], panels.at[8 * z], zw_s.at[z], zw_r.at[z], {"fsdp": zpeer[z]}) for z in range(1, ZN)
    ]
    z_grads = [copy(zg.at[0], zg.at[z], zg_s.at[z], zg_r.at[z], {"fsdp": zpeer[z]}) for z in range(1, ZN)]

    def send_own(z):
        if z:
            z_weights[z - 1].wait_recv()
        for k in (0, 2, 1, 3, 4, 5):
            moves[z][k].start()

    def forward(z):
        for k, onward in ((0, (6, 8)), (2, (7, 11)), (1, (9,)), (3, (10,))):
            moves[z][k].wait_recv()
            for other in onward:
                moves[z][other].start()

    def share(z):
        for k, other in ((6, 12), (7, 13)):
            moves[z][k].wait_recv()
            moves[z][other].start()

    def gathered(z):
        for k in (4, 5, 8, 9, 10, 11, 12, 13):
            moves[z][k].wait_recv()

    send_own(0)
    for one in z_weights:
        one.start()

    ev_copy.wait()
    for t in range(8):
        evt[t * depth:(t + 1) * depth, :] = ev[:, t * depth:(t + 1) * depth].T

    def project(r):
        start = pl.multiple_of(peer[r] * depth, depth)
        return mm(ev[:, pl.ds(start, depth)], panels[r])

    forward(0)
    send_own(1)
    acc = project(0)
    acc += project(2)
    acc += project(4)
    share(0)
    acc += project(6)
    gathered(0)
    for r in (1, 3, 5, 7):
        acc += project(r)

    proj = acc.astype(BF)
    q, k, v = proj[:, 0:128], proj[:, 128:256], proj[:, 256:384]

    def exchange(buf, ssem, rsem):
        sends = [copy(buf.at[0], buf.at[r], ssem.at[r], rsem.at[r], {"ctx": peer[r]}) for r in (6, 7, 2, 4, 3, 5, 1)]
        for one in sends:
            one.start()
        return sends

    st1[0] = mm(k, v, 0, 0).astype(BF)
    sends1 = exchange(st1, st1_s, st1_r)
    f00 = jnp.where(mask_ref[0, 0] > 0, 1.0, 0.0)
    f10 = jnp.where(mask_ref[1, 0] > 0, 1.0, 0.0)
    f11 = jnp.where(mask_ref[1, 1] > 0, 1.0, 0.0)
    size = 2 * TILE
    ri = lax.broadcasted_iota(jnp.int32, (size, size), 0)
    ci = lax.broadcasted_iota(jnp.int32, (size, size), 1)
    factor = jnp.where(ri >= TILE, jnp.where(ci >= TILE, f11, f10), f00)
    allowed = jnp.where(ci <= ri, factor, 0.0)
    mixing = (mm(q, k, 1, 1) * allowed).astype(BF)
    mixture = mm(mixing, v)
    up = cot_ref[...].astype(F32)
    forward(1)
    send_own(2)
    for one in sends1:
        one.wait_recv()
    carried = init_ref[0]
    for r in range(1, 8):
        carried += jnp.where(peer[r] < me, 1.0, 0.0) * st1[r].astype(F32)
    carried_bf = carried.astype(BF)
    mixture = mixture + mm(q, carried_bf)
    inv = lax.rsqrt(jnp.mean(mixture * mixture, axis=-1, keepdims=True) + epsilon)
    att_ref[...] = (mixture * inv).astype(BF)
    mg = (inv * up - mixture * (inv * inv * inv) * jnp.mean(up * mixture, axis=-1, keepdims=True)).astype(BF)
    st2[0] = mm(q, mg, 0, 0).astype(BF)
    sends2 = exchange(st2, st2_s, st2_r)
    share(1)
    sgrad = (mm(mg, v, 1, 1) * allowed).astype(BF)
    q_part = (mm(sgrad, k) + mm(mg, carried_bf, 1, 1)).astype(BF)
    k_local = mm(sgrad, q, 0, 0)
    v_local = mm(mixing, mg, 0, 0)
    for one in sends2:
        one.wait_recv()
    later = jnp.zeros((HDIM, HDIM), F32)
    for r in range(1, 8):
        later += jnp.where(peer[r] > me, 1.0, 0.0) * st2[r].astype(F32)
    later_bf = later.astype(BF)
    k_part = (k_local + mm(v, later_bf, 1, 1)).astype(BF)
    v_part = (v_local + mm(k, later_bf)).astype(BF)
    grads = jnp.concatenate([q_part, k_part, v_part], axis=1)

    zg[0] = grads
    for one in z_grads:
        one.start()

    def weight_term(r):
        start = pl.multiple_of(peer[r] * depth, depth)
        return mm(evt[pl.ds(start, depth), :], grads)

    sib = [copy(sib_out.at[i], sib_in.at[i], rs_s.at[i], rs_r.at[i], {"ctx": peer[1]}) for i in range(4)]
    to_x = {"ctx": peer[2]}
    to_y = {"ctx": peer[4]}
    dx = copy(piece.at[3, rows[0]], xd, rs_s.at[4], rs_r.at[4], to_x)
    dy = copy(piece.at[3, rows[1]], yd, rs_s.at[5], rs_r.at[5], to_y)
    px0 = copy(piece.at[1, rows[0]], xr.at[rows[0]], rs_s.at[6], rs_r.at[6], to_x)
    px1 = copy(piece.at[1, rows[1]], xr.at[rows[1]], rs_s.at[7], rs_r.at[7], to_x)
    py0 = copy(piece.at[2, rows[0]], yr.at[rows[0]], rs_s.at[8], rs_r.at[8], to_y)
    py1 = copy(piece.at[2, rows[1]], yr.at[rows[1]], rs_s.at[9], rs_r.at[9], to_y)

    def rs_step0():
        for i in (3, 1, 2, 0):
            sib_out[i] = weight_term(2 * i + 1).astype(BF)
            sib[i].start()

    def rs_step1():
        for i in (3, 1, 2, 0):
            term = weight_term(2 * i)
            sib[i].wait_recv()
            piece[i] = (term + sib_in[i].astype(F32)).astype(BF)
            if i == 3:
                dx.start()
                dy.start()
            if i == 1:
                px0.start()
            if i == 2:
                py1.start()

    def rs_step2():
        dx.wait_recv()
        piece[2, rows[0]] = (piece[2, rows[0]].astype(F32) + xd[...].astype(F32)).astype(BF)
        py0.start()
        dy.wait_recv()
        piece[1, rows[1]] = (piece[1, rows[1]].astype(F32) + yd[...].astype(F32)).astype(BF)
        px1.start()

    def rs_step3():
        for one in (px0, py1, px1, py0):
            one.wait_recv()
        total = (piece[0].astype(F32) + xr[...].astype(F32) + yr[...].astype(F32)).astype(BF)
        gq_ref[...] = total[:, 0:128]
        gk_ref[...] = total[:, 128:256]
        gv_ref[...] = total[:, 256:384]

    def add_group(z, last=False):
        theirs = zg[z]
        for r in range(8):
            term = mm(theirs, panels[8 * z + r], 1, 1)
            if z:
                term = acc_ref[r] + term
            if last:
                eg_ref[:, pl.ds(pl.multiple_of(peer[r] * depth, depth), depth)] = term.astype(BF)
            else:
                acc_ref[r] = term

    rs_step0()
    forward(2)
    send_own(3)
    rs_step1()
    add_group(0)
    share(2)
    rs_step2()
    gathered(1)
    z_grads[0].wait_recv()
    add_group(1)
    forward(3)
    share(3)
    gathered(2)
    z_grads[1].wait_recv()
    add_group(2)
    rs_step3()
    gathered(3)
    z_grads[2].wait_recv()
    add_group(3, True)

    for one in sum(moves, []) + z_weights + z_grads + sends1 + sends2 + sib:
        one.wait_send()
    for one in (dx, dy, px0, px1, py0, py1):
        one.wait_send()


def fused(events, tile_mask, initial_state, w_query, w_key, w_value, cotangent):
    tokens, width = events.shape
    depth, head = w_query.shape
    half = depth // 2
    wide = 3 * head
    vm = pl.BlockSpec(memory_space=pltpu.VMEM)
    dma = pltpu.SemaphoreType.DMA
    return pl.pallas_call(
        fused_kernel,
        out_shape=(
            jax.ShapeDtypeStruct((tokens, head), BF),
            jax.ShapeDtypeStruct((tokens, width), BF),
            jax.ShapeDtypeStruct((depth, head), BF),
            jax.ShapeDtypeStruct((depth, head), BF),
            jax.ShapeDtypeStruct((depth, head), BF),
        ),
        in_specs=[
            pl.BlockSpec(memory_space=pl.ANY),
            pl.BlockSpec(memory_space=pltpu.SMEM),
            vm, vm, vm, vm, vm,
        ],
        out_specs=(vm, vm, vm, vm, vm),
        scratch_shapes=[
            pltpu.VMEM((tokens, width), BF),
            pltpu.VMEM((width, tokens), BF),
            pltpu.VMEM((8 * ZN, depth, wide), BF),
            pltpu.VMEM((8, head, head), BF),
            pltpu.VMEM((8, head, head), BF),
            pltpu.VMEM((ZN, tokens, wide), BF),
            pltpu.VMEM((8, tokens, depth), F32),
            pltpu.VMEM((4, depth, wide), BF),
            pltpu.VMEM((4, depth, wide), BF),
            pltpu.VMEM((4, depth, wide), BF),
            pltpu.VMEM((half, wide), BF),
            pltpu.VMEM((half, wide), BF),
            pltpu.VMEM((depth, wide), BF),
            pltpu.VMEM((depth, wide), BF),
            dma(()),
            dma((14 * ZN,)), dma((14 * ZN,)),
            dma((8,)), dma((8,)), dma((8,)), dma((8,)),
            dma((10,)), dma((10,)),
            dma((ZN,)), dma((ZN,)), dma((ZN,)), dma((ZN,)),
        ],
        compiler_params=pltpu.CompilerParams(
            collective_id=0, has_side_effects=True, vmem_limit_bytes=56 * 1024 * 1024
        ),
        cost_estimate=pl.CostEstimate(
            flops=2 * tokens * width * wide * 3, bytes_accessed=6 * tokens * width, transcendentals=tokens
        ),
    )(events, tile_mask, initial_state, w_query, w_key, w_value, cotangent)


def solution(mesh):
    on_grid = mesh.shape["ctx"] == 8 and mesh.shape["fsdp"] == 4
    placed = (
        P("ctx", None),
        P("ctx", None),
        P("fsdp", None, None),
        P("ctx", "fsdp"),
        P("ctx", "fsdp"),
        P("ctx", "fsdp"),
        P("ctx", "fsdp"),
    )
    return jax.shard_map(
        fused if on_grid else on_device,
        mesh=mesh,
        in_specs=placed,
        out_specs=(
            P("ctx", "fsdp"),
            P("ctx", None),
            P("ctx", "fsdp"),
            P("ctx", "fsdp"),
            P("ctx", "fsdp"),
        ),
        check_vma=False,
    )
```
